32 devices in a mesh: groups: 2 (over x), clus: 16 (over z, y, core).
Axes of the slice: x: 2, y: 2, z: 4, core: 2. Of those that a mesh axis runs over, the one named last changes fastest.
Arguments:
- mesh_current: float32 [2, 131072], P(None, ('groups', 'clus')), parts along dimension 1, may hold values from -6 to 6
- branch_entry: int32 [2, 262144], P(None, ('groups', 'clus')), parts along dimension 1, may hold values from 0 to 6143, as said below
- branch_sign: int32 [2, 262144], P(None, ('groups', 'clus')), parts along dimension 1, may hold values from 0 to 1
- need_slots: int32 [512, 128], P(('groups', 'clus')), parts along dimension 0, may hold values from -1 to 4095, as said below
- resistance: float32 [262144], P(('groups', 'clus')), parts along dimension 0, may hold values from 0.3 to 3
- near_blocks: bfloat16 [2048, 4, 128, 128], P(('groups', 'clus')), parts along dimension 0, may hold values from -0.25 to 0.25
- near_source: int32 [2048, 4], P(('groups', 'clus')), parts along dimension 0, may hold values from 0 to 63
- basis_in: bfloat16 [2048, 32, 128], P(('groups', 'clus')), parts along dimension 0, may hold values from -0.5 to 0.5
- coupling: bfloat16 [2048, 16, 32, 32], P(('groups', 'clus')), parts along dimension 0, may hold values from -0.25 to 0.25
- basis_out: bfloat16 [2048, 32, 128], P(('groups', 'clus')), parts along dimension 0, may hold values from -1 to 1
- admissible: int32 [2048, 16], P(('groups', 'clus')), parts along dimension 0, may hold values from 0 to 1023, as said below
- port_mesh: int32 [128], P('groups'), parts along dimension 0, may hold values from 0 to 65535, as said below
- port_coupling: float32 [2, 64, 64], replicated, may hold values from -0.75 to 0.75
Outputs:
- mesh_voltage: float32 [2, 131072], P(None, ('groups', 'clus')), parts along dimension 1
The draws below stay inside these ranges and needn't reach their ends.
There are 2 independent parts, one for each index of `groups`. The reference program is written for one: setup_inputs(seed, part) draws one part's arguments, and reference() takes and returns one part's arrays. A program takes and returns all parts, laid end to end along the dimension named above; an argument that names none is the same for every part. Nothing has to cross between parts.
Inputs may be any that keep to these rules, and one draw needn't show every extreme that they name: `need_slots`: row d * 16 + p holds distinct meshes of device p, counted from 0 within it, in its first slots and -1 in the rest. Row d * 16 + d is all -1; row d * 16 + (d + 1) % 16 has no -1. `branch_entry`: A value below 4096 is a mesh of the branch's own device d. Any other value is 4096 + p * 128 + s with p != d and slot s of row d * 16 + p of need_slots not -1. `admissible`: entry k of row t is (t + k * 64 + o) % 1024 with 1 <= o < 64; the entries of a row are distinct and never t. `port_mesh`: distinct meshes.
All inputs are finite; a program needn't handle non-finite values.
Results may differ from the reference program's by a relative error of at most 0.0021.
Values may be sent and summed in bfloat16 or wider, within the bound.
A program may use at most 320 MiB of HBM per device.

```python
import math
import jax
import jax.numpy as jnp
from jax import lax

TILE_SIZE = 128
FAR_RANK = 32
NEAR_COUNT = 4
FAR_COUNT = 16
ENTRIES = 2
SLOT_COUNT = 128
PORT_COUNT = 64
TILE_DEV = 64
BRANCH_DEV = 8192
MESH_DEV = 4096
TILES = 1024
BRANCHES = 131072
MESHES = 65536
N_CLUS = 16


def slot_counts(key):
    drawn_counts = jax.random.randint(jax.random.fold_in(key, 11), (N_CLUS, N_CLUS), 1, SLOT_COUNT + 1)
    device_rows = jnp.arange(N_CLUS, dtype=jnp.int32)
    filled = device_rows[None, :] == (device_rows[:, None] + 1) % N_CLUS
    counts = jnp.where(filled, SLOT_COUNT, drawn_counts)
    return jnp.where(device_rows[:, None] == device_rows[None, :], 0, counts).astype(jnp.int32)


def first_meshes(one_key):
    return jax.random.permutation(one_key, MESH_DEV)[:SLOT_COUNT].astype(jnp.int32)


def draw_need_slots(key, part):
    counts = slot_counts(key).reshape(-1)
    mesh_keys = jax.random.split(jax.random.fold_in(key, 12), N_CLUS * N_CLUS)
    chosen = jax.vmap(first_meshes)(mesh_keys)
    places = jnp.arange(SLOT_COUNT, dtype=jnp.int32)
    return jnp.where(places[None, :] < counts[:, None], chosen, -1).astype(jnp.int32)


def draw_branch_entry(key, part):
    counts = slot_counts(key)
    entry_shape = (ENTRIES, BRANCHES)
    owner_device = jnp.broadcast_to(jnp.arange(BRANCHES, dtype=jnp.int32) // BRANCH_DEV, entry_shape)
    remote = jax.random.randint(jax.random.fold_in(key, 21), entry_shape, 0, 4) == 0
    peer_step = jax.random.randint(jax.random.fold_in(key, 22), entry_shape, 1, N_CLUS)
    peer = (owner_device + peer_step) % N_CLUS
    filled = counts[owner_device, peer]
    slot_place = jax.random.randint(jax.random.fold_in(key, 23), entry_shape, 0, filled)
    local_mesh = jax.random.randint(jax.random.fold_in(key, 24), entry_shape, 0, MESH_DEV)
    forced = (jnp.arange(BRANCHES, dtype=jnp.int32)[None, :] % BRANCH_DEV == 0) & (jnp.arange(ENTRIES, dtype=jnp.int32)[:, None] == ENTRIES - 1)
    peer = jnp.where(forced, (owner_device + 1) % N_CLUS, peer)
    slot_place = jnp.where(forced, SLOT_COUNT - 1, slot_place)
    remote = remote | forced
    return jnp.where(remote, MESH_DEV + peer * SLOT_COUNT + slot_place, local_mesh).astype(jnp.int32)


def draw_admissible(key, part):
    band_width = TILES // FAR_COUNT
    band_offset = jax.random.randint(jax.random.fold_in(key, 41), (TILES, FAR_COUNT), 1, band_width)
    tile_rows = jnp.arange(TILES, dtype=jnp.int32)[:, None]
    band_index = jnp.arange(FAR_COUNT, dtype=jnp.int32)[None, :]
    return ((tile_rows + band_index * band_width + band_offset) % TILES).astype(jnp.int32)


def draw_port_mesh(key, part):
    return jax.random.permutation(jax.random.fold_in(key, 51), MESHES)[:PORT_COUNT].astype(jnp.int32)


def plant(result, rng, smallest, largest):
    place = [jax.random.randint(jax.random.fold_in(rng, axis), (), 0, length) for axis, length in enumerate(result.shape)]
    longest = result.shape.index(max(result.shape))
    beside = place[:longest] + [(place[longest] + 1) % result.shape[longest]] + place[longest + 1:]
    return result.at[tuple(place)].set(smallest).at[tuple(beside)].set(largest)


def block_levels(key, extent, cuts, least, largest):
    factor_of, own = 1.0, jax.random.fold_in(key, 6)
    for dim, shards_of in cuts:
        steps = jnp.exp(jax.random.uniform(jax.random.fold_in(own, dim), (shards_of,), jnp.float32, least / len(cuts), largest / len(cuts)))
        factor_of = factor_of * jnp.repeat(steps, extent[dim] // shards_of).reshape([-1 if axis == dim else 1 for axis in range(len(extent))])
    return factor_of


def scatter_about(own_key, dims, spread, limit, pieces=(), kind=jnp.bfloat16):
    result = jax.random.normal(own_key, dims, jnp.float32) * spread
    if len(pieces) > 0:
        result = block_levels(own_key, dims, pieces, -0.22, 0.18) * result
    return jnp.clip(result, min=-limit, max=limit).astype(kind)


def setup_inputs(seed: int = 0, part: int = 0) -> dict:
    seeds = jax.random.split(jax.random.key(seed), 14)
    part_keys = jax.random.split(jax.random.fold_in(seeds[13], part), 14)
    return {
        "mesh_current": scatter_about(part_keys[0], (2, MESHES), 1.0, 6.0, ((1, 16),), jnp.float32),
        "branch_entry": draw_branch_entry(jax.random.fold_in(jax.random.fold_in(seeds[13], part), 71), part),
        "branch_sign": plant(jax.random.randint(part_keys[2], (ENTRIES, BRANCHES), 0, 2), jax.random.fold_in(part_keys[2], 1), 0, 1).astype(jnp.int32),
        "need_slots": draw_need_slots(jax.random.fold_in(jax.random.fold_in(seeds[13], part), 71), part),
        "resistance": jnp.clip(jnp.exp(math.log(3.0) - 2.3025851 * jax.random.uniform(part_keys[4], (BRANCHES,), jnp.float32) ** block_levels(part_keys[4], (BRANCHES,), ((0, 16),), -0.2, 0.2)), 0.3, 3.0),
        "near_blocks": scatter_about(part_keys[5], (TILES, NEAR_COUNT, TILE_SIZE, TILE_SIZE), (NEAR_COUNT * TILE_SIZE) ** -0.5, 0.25, ((0, 16),)),
        "near_source": plant(jax.random.randint(part_keys[6], (TILES, NEAR_COUNT), 0, TILE_DEV), jax.random.fold_in(part_keys[6], 1), 0, TILE_DEV - 1).astype(jnp.int32),
        "basis_in": scatter_about(part_keys[7], (TILES, FAR_RANK, TILE_SIZE), TILE_SIZE ** -0.5, 0.5, ((0, 16),)),
        "coupling": scatter_about(part_keys[8], (TILES, FAR_COUNT, FAR_RANK, FAR_RANK), (FAR_COUNT * FAR_RANK) ** -0.5, 0.25, ((0, 16),)),
        "basis_out": scatter_about(part_keys[9], (TILES, FAR_RANK, TILE_SIZE), FAR_RANK ** -0.5, 1.0, ((0, 16),)),
        "admissible": draw_admissible(jax.random.fold_in(jax.random.fold_in(seeds[13], part), 71), part),
        "port_mesh": draw_port_mesh(jax.random.fold_in(jax.random.fold_in(seeds[13], part), 71), part),
        "port_coupling": scatter_about(seeds[12], (2, PORT_COUNT, PORT_COUNT), PORT_COUNT ** -0.5, 0.75, (), jnp.float32),
    }


def near_part(block):
    blocks, source, inputs = block
    gathered = inputs[:, source]
    return jnp.einsum("tkij,ctkj->cti", blocks.astype(jnp.float32), gathered.astype(jnp.float32))


def segment_one(values, segment_ids):
    return jax.ops.segment_sum(values, segment_ids, num_segments=MESHES)


def reference(mesh_current, branch_entry, branch_sign, need_slots, resistance, near_blocks, near_source, basis_in, coupling, basis_out, admissible, port_mesh, port_coupling):
    devices = jnp.arange(N_CLUS, dtype=jnp.int32)
    table_width = MESH_DEV + N_CLUS * SLOT_COUNT
    needed = jnp.maximum(need_slots, 0).reshape(N_CLUS, N_CLUS * SLOT_COUNT)
    owner_base = jnp.repeat(devices * MESH_DEV, SLOT_COUNT)
    slot_mesh = needed + owner_base[None, :]
    own_mesh = devices[:, None] * MESH_DEV + jnp.arange(MESH_DEV, dtype=jnp.int32)[None, :]
    lookup_table = jnp.concatenate([own_mesh, slot_mesh], axis=1).reshape(-1)
    entries = branch_entry.reshape(ENTRIES, N_CLUS, BRANCH_DEV)
    flat_index = (devices[None, :, None] * table_width + entries).astype(jnp.int32)
    incident = lookup_table[flat_index].reshape(ENTRIES, BRANCHES)
    orient = (2 * branch_sign - 1).astype(jnp.float32)
    branch_current = jnp.sum(orient[None] * mesh_current[:, incident], axis=1)
    branch_input = branch_current.astype(jnp.bfloat16).reshape(2, TILES, TILE_SIZE)
    by_device = jnp.transpose(branch_input.reshape(2, N_CLUS, TILE_DEV, TILE_SIZE), (1, 0, 2, 3))
    near = lax.map(near_part, (near_blocks.reshape(N_CLUS, TILE_DEV, NEAR_COUNT, TILE_SIZE, TILE_SIZE), near_source.reshape(N_CLUS, TILE_DEV, NEAR_COUNT), by_device))
    near_field = jnp.transpose(near, (1, 0, 2, 3)).reshape(2, TILES, TILE_SIZE)
    far_coeff = jnp.einsum("tri,cti->ctr", basis_in.astype(jnp.float32), branch_input.astype(jnp.float32)).astype(jnp.bfloat16)
    picked = far_coeff[:, admissible]
    far_mixed = jnp.einsum("tkrq,ctkq->ctr", coupling.astype(jnp.float32), picked.astype(jnp.float32)).astype(jnp.bfloat16)
    far_field = jnp.einsum("tri,ctr->cti", basis_out.astype(jnp.float32), far_mixed.astype(jnp.float32))
    reactive = (near_field + far_field).reshape(2, BRANCHES)
    branch_voltage = resistance[None, :] * branch_current + jnp.stack([-reactive[1], reactive[0]])
    contributions = (orient[None] * branch_voltage[:, None, :]).reshape(2, -1)
    mesh_voltage = jax.vmap(segment_one, in_axes=(0, None))(contributions, incident.reshape(-1))
    port_current = mesh_current[:, port_mesh]
    high = lax.Precision.HIGHEST
    real_part = jnp.dot(port_coupling[0], port_current[0], precision=high) - jnp.dot(port_coupling[1], port_current[1], precision=high)
    imag_part = jnp.dot(port_coupling[0], port_current[1], precision=high) + jnp.dot(port_coupling[1], port_current[0], precision=high)
    mesh_voltage = mesh_voltage.at[:, port_mesh].add(jnp.stack([real_part, imag_part]))
    return mesh_voltage
```

```python
import functools

import jax
import jax.numpy as jnp
from jax import lax
from jax.experimental import pallas as pl
from jax.experimental.pallas import tpu as pltpu
from jax.sharding import PartitionSpec as P

LANES = 128
CHUNK = 1024
VMEM_LIMIT = 48 * 1024 * 1024
NT = (((1,), (1,)), ((), ()))


def exchange_kernel(peers, gather, x_ref, o_ref, send_sem, recv_sem, own_sem):
    me = lax.axis_index("clus")

    def peer_at(step):
        return lax.rem(me + step, peers)

    def copy_at(step):
        peer = peer_at(step)
        return pltpu.make_async_remote_copy(
            src_ref=x_ref if gather else x_ref.at[peer],
            dst_ref=o_ref.at[me],
            send_sem=send_sem.at[step],
            recv_sem=recv_sem.at[step],
            device_id={"clus": peer},
            device_id_type=pl.DeviceIdType.MESH,
        )

    barrier = pltpu.get_barrier_semaphore()

    @pl.loop(1, peers)
    def _(step):
        pl.semaphore_signal(
            barrier, inc=1, device_id={"clus": peer_at(step)}, device_id_type=pl.DeviceIdType.MESH
        )

    own = pltpu.make_async_copy(x_ref if gather else x_ref.at[me], o_ref.at[me], own_sem)
    own.start()
    pl.semaphore_wait(barrier, peers - 1)

    @pl.loop(1, peers)
    def _(step):
        copy_at(step).start()

    own.wait()

    @pl.loop(1, peers)
    def _(step):
        copy_at(step).wait()


def exchange(x, peers, collective_id, gather=False):
    shape = (peers,) + (x.shape if gather else x.shape[1:])
    return pl.pallas_call(
        functools.partial(exchange_kernel, peers, gather),
        out_shape=jax.ShapeDtypeStruct(shape, x.dtype),
        in_specs=[pl.BlockSpec(memory_space=pltpu.VMEM)],
        out_specs=pl.BlockSpec(memory_space=pltpu.VMEM),
        scratch_shapes=[
            pltpu.SemaphoreType.DMA((peers,)),
            pltpu.SemaphoreType.DMA((peers,)),
            pltpu.SemaphoreType.DMA,
        ],
        compiler_params=pltpu.CompilerParams(collective_id=collective_id, has_side_effects=True),
    )(x)


def split(value):
    high = value.astype(jnp.bfloat16).astype(jnp.float32)
    return high, value - high


def lanes_one_hot(index):
    low = index & (LANES - 1)
    rows = lax.broadcasted_iota(jnp.int32, (LANES, index.shape[1]), 0)
    return jnp.where(rows == low, 1.0, 0.0).astype(jnp.bfloat16)


def rows_mask(index, rows):
    return lax.broadcasted_iota(jnp.int32, (rows, index.shape[1]), 0) == (index >> 7)


def lookup_operand(tables):
    high, low = split(jnp.concatenate(tables, axis=0))
    return jnp.concatenate([high.astype(jnp.bfloat16), low.astype(jnp.bfloat16)], axis=1)


def look_up(operand, index, rows):
    hot = lanes_one_hot(index)
    found = jnp.dot(
        operand, jnp.concatenate([hot, hot], axis=0), preferred_element_type=jnp.float32
    )
    mask = rows_mask(index, rows)
    return [
        jnp.sum(jnp.where(mask, found[c * rows : (c + 1) * rows], 0.0), axis=0, keepdims=True)
        for c in range(2)
    ]


def sums(values, index, rows):
    hot = lanes_one_hot(index)
    mask = rows_mask(index, rows)
    parts = [split(value) for value in values]
    spread = [
        jnp.where(mask, parts[c][part], 0.0).astype(jnp.bfloat16)
        for part in range(2)
        for c in range(2)
    ]
    made = lax.dot_general(
        jnp.concatenate(spread, axis=0), hot, NT, preferred_element_type=jnp.float32
    )
    return made[: 2 * rows] + made[2 * rows :]


def row_of(ref, row, peers):
    return jnp.concatenate([ref[p, row : row + 1, :] for p in range(peers)], axis=1)


def answer_kernel(peers, mesh_rows, current_ref, asked_ref, port_ref, o_ref):
    operand = lookup_operand([current_ref[0], current_ref[1]])
    o_ref[...] = jnp.zeros_like(o_ref)
    asked = look_up(operand, row_of(asked_ref, 0, peers), mesh_rows)
    ports = look_up(operand, port_ref[...], mesh_rows)
    for p in range(peers):
        for c in range(2):
            o_ref[p, c : c + 1, :] = asked[c][:, p * LANES : (p + 1) * LANES]
            o_ref[p, 2 + c : 3 + c, :] = ports[c]


def branch_kernel(
    peers, rows, current_ref, remote_ref, entry_ref, sign_ref, basis_ref, flow_ref, coeff_ref
):
    operand = lookup_operand(
        [
            part
            for c in range(2)
            for part in [current_ref[c]] + [remote_ref[p, c : c + 1, :] for p in range(peers)]
        ]
    )

    @pl.loop(0, entry_ref.shape[1] // CHUNK)
    def _(step):
        columns = pl.ds(pl.multiple_of(step * CHUNK, CHUNK), CHUNK)
        total = [0.0, 0.0]
        for k in range(entry_ref.shape[0]):
            orient = (2 * sign_ref[k : k + 1, columns] - 1).astype(jnp.float32)
            found = look_up(operand, entry_ref[k : k + 1, columns], rows)
            total = [total[c] + orient * found[c] for c in range(2)]
        tiles = CHUNK // LANES
        for c in range(2):
            flow_ref[c, pl.ds(pl.multiple_of(step * tiles, tiles), tiles), :] = jnp.concatenate(
                [total[c][:, j * LANES : (j + 1) * LANES] for j in range(tiles)], axis=0
            )

    tile_dev = flow_ref.shape[1]
    rank = basis_ref.shape[0] // tile_dev
    width = 512
    for start in range(0, basis_ref.shape[0], width):
        basis = basis_ref[start : start + width, :]
        own = lax.broadcasted_iota(jnp.int32, (tile_dev, width), 0) == (
            lax.broadcasted_iota(jnp.int32, (tile_dev, width), 1) + start
        ) // rank
        for c in range(2):
            crossed = lax.dot_general(
                flow_ref[c].astype(jnp.bfloat16), basis, NT, preferred_element_type=jnp.float32
            )
            coeff_ref[c : c + 1, start : start + width] = jnp.sum(
                jnp.where(own, crossed, 0.0), axis=0, keepdims=True
            )


def collect_kernel(rows, voltage_ref, entry_ref, sign_ref, o_ref):
    o_ref[...] = jnp.zeros_like(o_ref)

    @pl.loop(0, entry_ref.shape[1] // CHUNK)
    def _(step):
        columns = pl.ds(pl.multiple_of(step * CHUNK, CHUNK), CHUNK)
        for k in range(entry_ref.shape[0]):
            orient = (2 * sign_ref[k : k + 1, columns] - 1).astype(jnp.float32)
            values = [orient * voltage_ref[c : c + 1, columns] for c in range(2)]
            o_ref[...] += sums(values, entry_ref[k : k + 1, columns], rows)


def finish_kernel(
    peers, rows, mesh_rows, sums_ref, arrived_ref, asked_ref, answer_ref, port_ref, z_ref, o_ref
):
    asked = row_of(asked_ref, 0, peers)
    arrived = sums([row_of(arrived_ref, c, peers) for c in range(2)], asked, mesh_rows)
    current = answer_ref[0]
    for p in range(1, peers):
        current = current + answer_ref[p]
    products = [
        lax.dot_general(
            current,
            z_ref[part],
            NT,
            precision=lax.Precision.HIGHEST,
            preferred_element_type=jnp.float32,
        )
        for part in range(2)
    ]
    real_part = products[0][2:3] - products[1][3:4]
    imag_part = products[0][3:4] + products[1][2:3]
    ports = sums([real_part, imag_part], port_ref[...], mesh_rows)
    for c in range(2):
        own = slice(c * mesh_rows, (c + 1) * mesh_rows)
        o_ref[c] = sums_ref[c * rows : c * rows + mesh_rows, :] + arrived[own] + ports[own]


def local_call(body, shapes, *arrays):
    return pl.pallas_call(
        body,
        out_shape=shapes,
        compiler_params=pltpu.CompilerParams(vmem_limit_bytes=VMEM_LIMIT),
    )(*arrays)


def f32(*shape):
    return jax.ShapeDtypeStruct(shape, jnp.float32)


def per_device(
    mesh_current,
    branch_entry,
    branch_sign,
    need_slots,
    resistance,
    near_blocks,
    near_source,
    basis_in,
    coupling,
    basis_out,
    admissible,
    port_mesh,
    port_coupling,
):
    peers = lax.axis_size("clus")
    mesh_dev = mesh_current.shape[1]
    branch_dev = branch_entry.shape[1]
    tile_dev, near_count, tile_width = near_blocks.shape[:3]
    rank = basis_in.shape[1]
    ports = port_mesh.shape[0]
    mesh_rows = mesh_dev // LANES
    rows = mesh_rows + peers
    current = mesh_current.reshape(2, mesh_rows, LANES)
    offset = lax.axis_index("clus") * mesh_dev
    port_position = jnp.pad(port_mesh, (0, LANES - ports), constant_values=-1)[None, :] - offset
    impedance = jnp.pad(port_coupling, ((0, 0), (0, LANES - ports), (0, LANES - ports)))

    asked = exchange(jnp.pad(need_slots[:, None, :], ((0, 0), (0, 7), (0, 0))), peers, 0)
    answer = exchange(
        local_call(
            functools.partial(answer_kernel, peers, mesh_rows),
            f32(peers, 8, LANES),
            current,
            asked,
            port_position,
        ),
        peers,
        1,
    )
    flow, coeff = local_call(
        functools.partial(branch_kernel, peers, rows),
        [f32(2, tile_dev, LANES), f32(2, tile_dev * rank)],
        current,
        answer,
        branch_entry,
        branch_sign,
        basis_in.reshape(tile_dev * rank, tile_width),
    )
    branch_input = flow.astype(jnp.bfloat16)
    mine = coeff.astype(jnp.bfloat16).reshape(-1, LANES)
    all_coeff = exchange(mine, peers, 2, gather=True)

    near_hot = jax.nn.one_hot(near_source.reshape(-1), tile_dev, dtype=jnp.bfloat16)
    near_input = jnp.einsum(
        "ns,csj->cnj", near_hot, branch_input, preferred_element_type=jnp.bfloat16
    ).reshape(2, tile_dev, near_count, tile_width)
    near_field = jnp.einsum(
        "tkij,ctkj->cti", near_blocks, near_input, preferred_element_type=jnp.float32
    )
    table = all_coeff.reshape(peers, 2, tile_dev, rank).transpose(0, 2, 1, 3)
    far_hot = jax.nn.one_hot(admissible.reshape(-1), peers * tile_dev, dtype=jnp.bfloat16)
    picked = jnp.dot(
        far_hot,
        table.reshape(peers * tile_dev, 2 * rank),
        preferred_element_type=jnp.bfloat16,
    ).reshape(tile_dev, -1, 2, rank)
    far_mixed = jnp.einsum(
        "tkrq,tkcq->ctr", coupling, picked, preferred_element_type=jnp.float32
    ).astype(jnp.bfloat16)
    far_field = jnp.einsum("tri,ctr->cti", basis_out, far_mixed, preferred_element_type=jnp.float32)
    reactive = near_field + far_field
    resistive = resistance.reshape(1, tile_dev, tile_width) * flow
    voltage = (resistive + jnp.stack([-reactive[1], reactive[0]])).reshape(2, branch_dev)

    totals = local_call(
        functools.partial(collect_kernel, rows),
        f32(2 * rows, LANES),
        voltage,
        branch_entry,
        branch_sign,
    )
    slots = totals.reshape(2, rows, LANES)[:, mesh_rows:].transpose(1, 0, 2)
    arrived = exchange(jnp.pad(slots, ((0, 0), (0, 6), (0, 0))), peers, 3)
    made = local_call(
        functools.partial(finish_kernel, peers, rows, mesh_rows),
        f32(2, mesh_rows, LANES),
        totals,
        arrived,
        asked,
        answer,
        port_position,
        impedance,
    )
    return made.reshape(2, mesh_dev)


def solution(mesh):
    in_specs = (
        P(None, ("groups", "clus")),
        P(None, ("groups", "clus")),
        P(None, ("groups", "clus")),
        P(("groups", "clus"), None),
        P(("groups", "clus")),
        P(("groups", "clus"), None, None, None),
        P(("groups", "clus"), None),
        P(("groups", "clus"), None, None),
        P(("groups", "clus"), None, None, None),
        P(("groups", "clus"), None, None),
        P(("groups", "clus"), None),
        P("groups"),
        P(),
    )
    out_specs = P(None, ("groups", "clus"))
    return jax.shard_map(
        per_device, mesh=mesh, in_specs=in_specs, out_specs=out_specs, check_vma=False
    )
```

```python
import functools

import jax
import jax.numpy as jnp
from jax import lax
from jax.experimental import pallas as pl
from jax.experimental.pallas import tpu as pltpu
from jax.sharding import PartitionSpec as P

LANES = 128
CHUNK = 1024
VMEM_LIMIT = 48 * 1024 * 1024
NT = (((1,), (1,)), ((), ()))


def exchange_kernel(peers, gather, work, x_ref, *refs):
    *work_ins, o_ref, send_sem, recv_sem, own_sem = refs
    if work is not None:
        *work_ins, o_ref, work_out, send_sem, recv_sem, own_sem, work_scratch = refs
    me = lax.axis_index("clus")

    def peer_at(step):
        return lax.rem(me + step, peers)

    def copy_at(step):
        peer = peer_at(step)
        return pltpu.make_async_remote_copy(
            src_ref=x_ref if gather else x_ref.at[peer],
            dst_ref=o_ref.at[me],
            send_sem=send_sem.at[step],
            recv_sem=recv_sem.at[step],
            device_id={"clus": peer},
            device_id_type=pl.DeviceIdType.MESH,
        )

    barrier = pltpu.get_barrier_semaphore()

    @pl.loop(1, peers)
    def _(step):
        pl.semaphore_signal(
            barrier, inc=1, device_id={"clus": peer_at(step)}, device_id_type=pl.DeviceIdType.MESH
        )

    own = pltpu.make_async_copy(x_ref if gather else x_ref.at[me], o_ref.at[me], own_sem)
    own.start()
    pl.semaphore_wait(barrier, peers - 1)

    @pl.loop(1, peers)
    def _(step):
        copy_at(step).start()

    own.wait()
    if work is not None:
        work(*work_ins, work_out, work_scratch)

    @pl.loop(1, peers)
    def _(step):
        copy_at(step).wait()


def exchange(x, peers, collective_id, gather=False, work=None, extra=(), made=(), scratch=()):
    shape = (peers,) + (x.shape if gather else x.shape[1:])
    vmem = pl.BlockSpec(memory_space=pltpu.VMEM)
    out = pl.pallas_call(
        functools.partial(exchange_kernel, peers, gather, work),
        out_shape=[jax.ShapeDtypeStruct(shape, x.dtype), *made],
        in_specs=[vmem] * (1 + len(extra)),
        out_specs=[vmem] * (1 + len(made)),
        scratch_shapes=[
            pltpu.SemaphoreType.DMA((peers,)),
            pltpu.SemaphoreType.DMA((peers,)),
            pltpu.SemaphoreType.DMA,
            *scratch,
        ],
        compiler_params=pltpu.CompilerParams(
            collective_id=collective_id, has_side_effects=True, vmem_limit_bytes=VMEM_LIMIT
        ),
    )(x, *extra)
    return out if made else out[0]


def near_work(flow_ref, source_ref, blocks_ref, near_ref, picked_ref):
    tile_dev, near_count = blocks_ref.shape[:2]
    count = source_ref.shape[0]
    hot = jnp.where(
        lax.broadcasted_iota(jnp.int32, (count, tile_dev), 1) == source_ref[...], 1.0, 0.0
    ).astype(jnp.bfloat16)
    for c in range(2):
        picked_ref[c] = jnp.dot(
            hot, flow_ref[c].astype(jnp.bfloat16), preferred_element_type=jnp.float32
        )

    @pl.loop(0, tile_dev // 8)
    def _(step):
        rows = []
        for j in range(8):
            tile = step * 8 + j
            total = 0.0
            for k in range(near_count):
                place = pl.ds(tile * near_count + k, 1)
                source = jnp.concatenate([picked_ref[0, place, :], picked_ref[1, place, :]], axis=0)
                total += lax.dot_general(
                    source.astype(jnp.bfloat16),
                    blocks_ref[tile, k],
                    NT,
                    preferred_element_type=jnp.float32,
                )
            rows.append(total)
        for c in range(2):
            near_ref[c, pl.ds(pl.multiple_of(step * 8, 8), 8), :] = jnp.concatenate(
                [row[c : c + 1] for row in rows], axis=0
            )


def split(value):
    high = value.astype(jnp.bfloat16).astype(jnp.float32)
    return high, value - high


def lanes_one_hot(index):
    low = index & (LANES - 1)
    rows = lax.broadcasted_iota(jnp.int32, (LANES, index.shape[1]), 0)
    return jnp.where(rows == low, 1.0, 0.0).astype(jnp.bfloat16)


def rows_mask(index, rows):
    return lax.broadcasted_iota(jnp.int32, (rows, index.shape[1]), 0) == (index >> 7)


def lookup_operand(tables):
    high, low = split(jnp.concatenate(tables, axis=0))
    return jnp.concatenate([high.astype(jnp.bfloat16), low.astype(jnp.bfloat16)], axis=1)


def look_up(operand, index, rows):
    hot = lanes_one_hot(index)
    found = jnp.dot(
        operand, jnp.concatenate([hot, hot], axis=0), preferred_element_type=jnp.float32
    )
    mask = rows_mask(index, rows)
    return [
        jnp.sum(jnp.where(mask, found[c * rows : (c + 1) * rows], 0.0), axis=0, keepdims=True)
        for c in range(2)
    ]


def sums(values, index, rows):
    hot = lanes_one_hot(index)
    mask = rows_mask(index, rows)
    parts = [split(value) for value in values]
    spread = [
        jnp.where(mask, parts[c][part], 0.0).astype(jnp.bfloat16)
        for part in range(2)
        for c in range(2)
    ]
    made = lax.dot_general(
        jnp.concatenate(spread, axis=0), hot, NT, preferred_element_type=jnp.float32
    )
    return made[: 2 * rows] + made[2 * rows :]


def row_of(ref, row, peers):
    return jnp.concatenate([ref[p, row : row + 1, :] for p in range(peers)], axis=1)


def answer_kernel(peers, mesh_rows, current_ref, asked_ref, port_ref, o_ref):
    operand = lookup_operand([current_ref[0], current_ref[1]])
    o_ref[...] = jnp.zeros_like(o_ref)
    asked = look_up(operand, row_of(asked_ref, 0, peers), mesh_rows)
    ports = look_up(operand, port_ref[...], mesh_rows)
    for p in range(peers):
        for c in range(2):
            o_ref[p, c : c + 1, :] = asked[c][:, p * LANES : (p + 1) * LANES]
            o_ref[p, 2 + c : 3 + c, :] = ports[c]


def branch_kernel(
    peers, rows, current_ref, remote_ref, entry_ref, sign_ref, basis_ref, flow_ref, coeff_ref
):
    operand = lookup_operand(
        [
            part
            for c in range(2)
            for part in [current_ref[c]] + [remote_ref[p, c : c + 1, :] for p in range(peers)]
        ]
    )

    @pl.loop(0, entry_ref.shape[1] // CHUNK)
    def _(step):
        columns = pl.ds(pl.multiple_of(step * CHUNK, CHUNK), CHUNK)
        total = [0.0, 0.0]
        for k in range(entry_ref.shape[0]):
            orient = (2 * sign_ref[k : k + 1, columns] - 1).astype(jnp.float32)
            found = look_up(operand, entry_ref[k : k + 1, columns], rows)
            total = [total[c] + orient * found[c] for c in range(2)]
        tiles = CHUNK // LANES
        for c in range(2):
            flow_ref[c, pl.ds(pl.multiple_of(step * tiles, tiles), tiles), :] = jnp.concatenate(
                [total[c][:, j * LANES : (j + 1) * LANES] for j in range(tiles)], axis=0
            )

    tile_dev = flow_ref.shape[1]
    rank = basis_ref.shape[0] // tile_dev
    flows = jnp.concatenate([flow_ref[0], flow_ref[1]], axis=0).astype(jnp.bfloat16)
    part = 8
    total = jnp.zeros((rank, 2 * tile_dev), jnp.float32)
    for start in range(0, tile_dev, part):
        crossed = lax.dot_general(
            basis_ref[start * rank : (start + part) * rank, :],
            flows,
            NT,
            preferred_element_type=jnp.float32,
        )
        lane = lax.broadcasted_iota(jnp.int32, (rank, 2 * tile_dev), 1) & (tile_dev - 1)
        for j in range(part):
            total += jnp.where(lane == start + j, crossed[j * rank : (j + 1) * rank], 0.0)
    coeff_ref[...] = total.astype(jnp.bfloat16)


def far_and_collect_kernel(
    peers,
    rows,
    coeff_ref,
    admissible_ref,
    coupling_ref,
    basis_ref,
    near_ref,
    flow_ref,
    resistance_ref,
    entry_ref,
    sign_ref,
    o_ref,
    picked_ref,
    voltage_ref,
):
    tile_dev, rank = basis_ref.shape[:2]
    far_count = coupling_ref.shape[1] // rank
    group = LANES // far_count
    held = coeff_ref[...].reshape(peers * rank, 2 * tile_dev)
    for start in range(0, admissible_ref.shape[1], 512):
        index = admissible_ref[:, start : start + 512]
        low = index & (tile_dev - 1)
        owner = index // tile_dev
        tile = lax.broadcasted_iota(jnp.int32, (2 * tile_dev, 512), 0)
        for c in range(2):
            hot = jnp.where(tile == low + c * tile_dev, 1.0, 0.0).astype(jnp.bfloat16)
            found = jnp.dot(held, hot, preferred_element_type=jnp.float32)
            total = jnp.zeros((rank, 512), jnp.float32)
            for p in range(peers):
                total += jnp.where(owner == p, found[p * rank : (p + 1) * rank], 0.0)
            for j in range(512 // LANES):
                picked_ref[start // LANES + j, :, c * LANES : (c + 1) * LANES] = total[
                    :, j * LANES : (j + 1) * LANES
                ].astype(jnp.bfloat16)
    spread = jnp.where(
        lax.broadcasted_iota(jnp.int32, (2 * LANES, group * LANES), 0) % LANES // far_count
        == lax.broadcasted_iota(jnp.int32, (2 * LANES, group * LANES), 1) // LANES,
        1.0,
        0.0,
    ).astype(jnp.bfloat16)

    @pl.loop(0, tile_dev // group)
    def _(step):
        picked = picked_ref[step]
        lane = lax.broadcasted_iota(jnp.int32, (rank, 2 * LANES), 1) & (LANES - 1)
        mixed = jnp.zeros((rank, 2 * LANES), jnp.float32)
        for j in range(group):
            crossed = jnp.dot(
                coupling_ref[step * group + j], picked, preferred_element_type=jnp.float32
            )
            for k in range(far_count):
                mixed += jnp.where(
                    lane == j * far_count + k, crossed[k * rank : (k + 1) * rank], 0.0
                )
        far = []
        for c in range(2):
            wide = jnp.dot(
                lookup_operand([mixed[:, c * LANES : (c + 1) * LANES]]),
                spread,
                preferred_element_type=jnp.float32,
            )
            wide = wide.astype(jnp.bfloat16).astype(jnp.float32)
            far.append(
                jnp.concatenate(
                    [
                        jnp.sum(
                            basis_ref[step * group + j].astype(jnp.float32)
                            * wide[:, j * LANES : (j + 1) * LANES],
                            axis=0,
                            keepdims=True,
                        )
                        for j in range(group)
                    ],
                    axis=0,
                )
            )
        place = pl.ds(pl.multiple_of(step * group, group), group)
        resistance = resistance_ref[place, :]
        reactive = [near_ref[c, place, :] + far[c] for c in range(2)]
        voltage_ref[0, place, :] = resistance * flow_ref[0, place, :] - reactive[1]
        voltage_ref[1, place, :] = resistance * flow_ref[1, place, :] + reactive[0]

    o_ref[...] = jnp.zeros_like(o_ref)

    @pl.loop(0, entry_ref.shape[1] // CHUNK)
    def _(step):
        columns = pl.ds(pl.multiple_of(step * CHUNK, CHUNK), CHUNK)
        tiles = CHUNK // LANES
        voltage = [
            voltage_ref[c, pl.ds(pl.multiple_of(step * tiles, tiles), tiles), :] for c in range(2)
        ]
        voltage = [
            jnp.concatenate([value[j : j + 1] for j in range(tiles)], axis=1) for value in voltage
        ]
        for k in range(entry_ref.shape[0]):
            orient = (2 * sign_ref[k : k + 1, columns] - 1).astype(jnp.float32)
            values = [orient * voltage[c] for c in range(2)]
            o_ref[...] += sums(values, entry_ref[k : k + 1, columns], rows)


def finish_kernel(
    peers, rows, mesh_rows, sums_ref, arrived_ref, asked_ref, answer_ref, port_ref, z_ref, o_ref
):
    asked = row_of(asked_ref, 0, peers)
    arrived = sums([row_of(arrived_ref, c, peers) for c in range(2)], asked, mesh_rows)
    current = answer_ref[0]
    for p in range(1, peers):
        current = current + answer_ref[p]
    products = [
        lax.dot_general(
            current,
            z_ref[part],
            NT,
            precision=lax.Precision.HIGHEST,
            preferred_element_type=jnp.float32,
        )
        for part in range(2)
    ]
    real_part = products[0][2:3] - products[1][3:4]
    imag_part = products[0][3:4] + products[1][2:3]
    ports = sums([real_part, imag_part], port_ref[...], mesh_rows)
    for c in range(2):
        own = slice(c * mesh_rows, (c + 1) * mesh_rows)
        o_ref[c] = sums_ref[c * rows : c * rows + mesh_rows, :] + arrived[own] + ports[own]


def local_call(body, shapes, *arrays, scratch=()):
    return pl.pallas_call(
        body,
        out_shape=shapes,
        scratch_shapes=list(scratch),
        compiler_params=pltpu.CompilerParams(vmem_limit_bytes=VMEM_LIMIT),
    )(*arrays)


def f32(*shape):
    return jax.ShapeDtypeStruct(shape, jnp.float32)


def per_device(
    mesh_current,
    branch_entry,
    branch_sign,
    need_slots,
    resistance,
    near_blocks,
    near_source,
    basis_in,
    coupling,
    basis_out,
    admissible,
    port_mesh,
    port_coupling,
):
    peers = lax.axis_size("clus")
    mesh_dev = mesh_current.shape[1]
    tile_dev, near_count, tile_width = near_blocks.shape[:3]
    rank = basis_in.shape[1]
    ports = port_mesh.shape[0]
    mesh_rows = mesh_dev // LANES
    rows = mesh_rows + peers
    current = mesh_current.reshape(2, mesh_rows, LANES)
    offset = lax.axis_index("clus") * mesh_dev
    port_position = jnp.pad(port_mesh, (0, LANES - ports), constant_values=-1)[None, :] - offset
    impedance = jnp.pad(port_coupling, ((0, 0), (0, LANES - ports), (0, LANES - ports)))

    asked = exchange(jnp.pad(need_slots[:, None, :], ((0, 0), (0, 7), (0, 0))), peers, 0)
    answer = exchange(
        local_call(
            functools.partial(answer_kernel, peers, mesh_rows),
            f32(peers, 8, LANES),
            current,
            asked,
            port_position,
        ),
        peers,
        1,
    )
    flow, coeff = local_call(
        functools.partial(branch_kernel, peers, rows),
        [f32(2, tile_dev, LANES), jax.ShapeDtypeStruct((rank, 2 * tile_dev), jnp.bfloat16)],
        current,
        answer,
        branch_entry,
        branch_sign,
        basis_in.reshape(tile_dev * rank, tile_width),
    )
    all_coeff, near_field = exchange(
        coeff,
        peers,
        2,
        gather=True,
        work=near_work,
        extra=(flow, near_source.reshape(-1, 1), near_blocks),
        made=(f32(2, tile_dev, LANES),),
        scratch=(pltpu.VMEM((2, tile_dev * near_count, LANES), jnp.float32),),
    )
    far_count = admissible.shape[1]
    totals = local_call(
        functools.partial(far_and_collect_kernel, peers, rows),
        f32(2 * rows, LANES),
        all_coeff,
        admissible.reshape(1, -1),
        coupling.reshape(tile_dev, far_count * rank, rank),
        basis_out,
        near_field,
        flow,
        resistance.reshape(tile_dev, tile_width),
        branch_entry,
        branch_sign,
        scratch=(
            pltpu.VMEM((tile_dev * far_count // LANES, rank, 2 * LANES), jnp.bfloat16),
            pltpu.VMEM((2, tile_dev, LANES), jnp.float32),
        ),
    )
    slots = totals.reshape(2, rows, LANES)[:, mesh_rows:].transpose(1, 0, 2)
    arrived = exchange(jnp.pad(slots, ((0, 0), (0, 6), (0, 0))), peers, 3)
    made = local_call(
        functools.partial(finish_kernel, peers, rows, mesh_rows),
        f32(2, mesh_rows, LANES),
        totals,
        arrived,
        asked,
        answer,
        port_position,
        impedance,
    )
    return made.reshape(2, mesh_dev)


def solution(mesh):
    in_specs = (
        P(None, ("groups", "clus")),
        P(None, ("groups", "clus")),
        P(None, ("groups", "clus")),
        P(("groups", "clus"), None),
        P(("groups", "clus")),
        P(("groups", "clus"), None, None, None),
        P(("groups", "clus"), None),
        P(("groups", "clus"), None, None),
        P(("groups", "clus"), None, None, None),
        P(("groups", "clus"), None, None),
        P(("groups", "clus"), None),
        P("groups"),
        P(),
    )
    out_specs = P(None, ("groups", "clus"))
    return jax.shard_map(
        per_device, mesh=mesh, in_specs=in_specs, out_specs=out_specs, check_vma=False
    )
```

```python
import functools

import jax
import jax.numpy as jnp
from jax import lax
from jax.experimental import pallas as pl
from jax.experimental.pallas import tpu as pltpu
from jax.sharding import PartitionSpec as P

LANES = 128
CHUNK = 1024
VMEM_LIMIT = 48 * 1024 * 1024
NT = (((1,), (1,)), ((), ()))


def exchange_kernel(peers, gather, work, x_ref, *refs):
    *work_ins, o_ref, send_sem, recv_sem, own_sem = refs
    if work is not None:
        *work_ins, o_ref, work_out, send_sem, recv_sem, own_sem, work_scratch = refs
    me = lax.axis_index("clus")

    def peer_at(step):
        return lax.rem(me + step, peers)

    def copy_at(step):
        peer = peer_at(step)
        return pltpu.make_async_remote_copy(
            src_ref=x_ref if gather else x_ref.at[peer],
            dst_ref=o_ref.at[me],
            send_sem=send_sem.at[step],
            recv_sem=recv_sem.at[step],
            device_id={"clus": peer},
            device_id_type=pl.DeviceIdType.MESH,
        )

    barrier = pltpu.get_barrier_semaphore()

    @pl.loop(1, peers)
    def _(step):
        pl.semaphore_signal(
            barrier, inc=1, device_id={"clus": peer_at(step)}, device_id_type=pl.DeviceIdType.MESH
        )

    own = pltpu.make_async_copy(x_ref if gather else x_ref.at[me], o_ref.at[me], own_sem)
    own.start()
    pl.semaphore_wait(barrier, peers - 1)

    @pl.loop(1, peers)
    def _(step):
        copy_at(step).start()

    own.wait()
    if work is not None:
        work(*work_ins, work_out, work_scratch)

    @pl.loop(1, peers)
    def _(step):
        copy_at(step).wait()


def exchange(x, peers, collective_id, gather=False, work=None, extra=(), made=(), scratch=()):
    shape = (peers,) + (x.shape if gather else x.shape[1:])
    vmem = pl.BlockSpec(memory_space=pltpu.VMEM)
    out = pl.pallas_call(
        functools.partial(exchange_kernel, peers, gather, work),
        out_shape=[jax.ShapeDtypeStruct(shape, x.dtype), *made],
        in_specs=[vmem] * (1 + len(extra)),
        out_specs=[vmem] * (1 + len(made)),
        scratch_shapes=[
            pltpu.SemaphoreType.DMA((peers,)),
            pltpu.SemaphoreType.DMA((peers,)),
            pltpu.SemaphoreType.DMA,
            *scratch,
        ],
        compiler_params=pltpu.CompilerParams(
            collective_id=collective_id, has_side_effects=True, vmem_limit_bytes=VMEM_LIMIT
        ),
    )(x, *extra)
    return out if made else out[0]


def near_work(flow_ref, source_ref, blocks_ref, near_ref, picked_ref):
    tile_dev, near_count = blocks_ref.shape[:2]
    count = source_ref.shape[0]
    hot = jnp.where(
        lax.broadcasted_iota(jnp.int32, (count, tile_dev), 1) == source_ref[...], 1.0, 0.0
    ).astype(jnp.bfloat16)
    for c in range(2):
        picked_ref[c] = jnp.dot(
            hot, flow_ref[c].astype(jnp.bfloat16), preferred_element_type=jnp.float32
        )

    @pl.loop(0, tile_dev // 8)
    def _(step):
        rows = []
        for j in range(8):
            tile = step * 8 + j
            total = 0.0
            for k in range(near_count):
                place = pl.ds(tile * near_count + k, 1)
                source = jnp.concatenate([picked_ref[0, place, :], picked_ref[1, place, :]], axis=0)
                total += lax.dot_general(
                    source.astype(jnp.bfloat16),
                    blocks_ref[tile, k],
                    NT,
                    preferred_element_type=jnp.float32,
                )
            rows.append(total)
        for c in range(2):
            near_ref[c, pl.ds(pl.multiple_of(step * 8, 8), 8), :] = jnp.concatenate(
                [row[c : c + 1] for row in rows], axis=0
            )


def split(value):
    high = value.astype(jnp.bfloat16).astype(jnp.float32)
    return high, value - high


def lanes_one_hot(index):
    low = index & (LANES - 1)
    rows = lax.broadcasted_iota(jnp.int32, (LANES, index.shape[1]), 0)
    return jnp.where(rows == low, 1.0, 0.0).astype(jnp.bfloat16)


def rows_mask(index, rows):
    return lax.broadcasted_iota(jnp.int32, (rows, index.shape[1]), 0) == (index >> 7)


def lookup_operand(tables):
    high, low = split(jnp.concatenate(tables, axis=0))
    return jnp.concatenate([high.astype(jnp.bfloat16), low.astype(jnp.bfloat16)], axis=1)


def look_up(operand, index, rows):
    hot = lanes_one_hot(index)
    found = jnp.dot(
        operand, jnp.concatenate([hot, hot], axis=0), preferred_element_type=jnp.float32
    )
    mask = rows_mask(index, rows)
    return [
        jnp.sum(jnp.where(mask, found[c * rows : (c + 1) * rows], 0.0), axis=0, keepdims=True)
        for c in range(2)
    ]


def sums(values, index, rows):
    hot = lanes_one_hot(index)
    mask = rows_mask(index, rows)
    parts = [split(value) for value in values]
    spread = [
        jnp.where(mask, parts[c][part], 0.0).astype(jnp.bfloat16)
        for part in range(2)
        for c in range(2)
    ]
    made = lax.dot_general(
        jnp.concatenate(spread, axis=0), hot, NT, preferred_element_type=jnp.float32
    )
    return made[: 2 * rows] + made[2 * rows :]


def row_of(ref, row, peers):
    return jnp.concatenate([ref[p, row : row + 1, :] for p in range(peers)], axis=1)


def answer_kernel(peers, mesh_rows, current_ref, asked_ref, port_ref, o_ref):
    operand = lookup_operand([current_ref[0], current_ref[1]])
    o_ref[...] = jnp.zeros_like(o_ref)
    asked = look_up(operand, row_of(asked_ref, 0, peers), mesh_rows)
    ports = look_up(operand, port_ref[...], mesh_rows)
    for p in range(peers):
        for c in range(2):
            o_ref[p, c : c + 1, :] = asked[c][:, p * LANES : (p + 1) * LANES]
            o_ref[p, 2 + c : 3 + c, :] = ports[c]


def branch_kernel(
    peers, rows, current_ref, remote_ref, entry_ref, sign_ref, basis_ref, flow_ref, coeff_ref
):
    operand = lookup_operand(
        [
            part
            for c in range(2)
            for part in [current_ref[c]] + [remote_ref[p, c : c + 1, :] for p in range(peers)]
        ]
    )

    @pl.loop(0, entry_ref.shape[1] // CHUNK)
    def _(step):
        columns = pl.ds(pl.multiple_of(step * CHUNK, CHUNK), CHUNK)
        total = [0.0, 0.0]
        for k in range(entry_ref.shape[0]):
            orient = (2 * sign_ref[k : k + 1, columns] - 1).astype(jnp.float32)
            found = look_up(operand, entry_ref[k : k + 1, columns], rows)
            total = [total[c] + orient * found[c] for c in range(2)]
        tiles = CHUNK // LANES
        for c in range(2):
            flow_ref[c, pl.ds(pl.multiple_of(step * tiles, tiles), tiles), :] = jnp.concatenate(
                [total[c][:, j * LANES : (j + 1) * LANES] for j in range(tiles)], axis=0
            )

    tile_dev = flow_ref.shape[1]
    rank = basis_ref.shape[0] // tile_dev
    flows = jnp.concatenate([flow_ref[0], flow_ref[1]], axis=0).astype(jnp.bfloat16)
    part = 8
    total = jnp.zeros((rank, 2 * tile_dev), jnp.float32)
    for start in range(0, tile_dev, part):
        crossed = lax.dot_general(
            basis_ref[start * rank : (start + part) * rank, :],
            flows,
            NT,
            preferred_element_type=jnp.float32,
        )
        lane = lax.broadcasted_iota(jnp.int32, (rank, 2 * tile_dev), 1) & (tile_dev - 1)
        for j in range(part):
            total += jnp.where(lane == start + j, crossed[j * rank : (j + 1) * rank], 0.0)
    coeff_ref[...] = total.astype(jnp.bfloat16)


def far_and_collect_kernel(
    peers,
    rows,
    coeff_ref,
    admissible_ref,
    coupling_ref,
    basis_ref,
    near_ref,
    flow_ref,
    resistance_ref,
    entry_ref,
    sign_ref,
    o_ref,
    picked_ref,
    mixed_ref,
    voltage_ref,
):
    tile_dev, rank = basis_ref.shape[:2]
    far_count = coupling_ref.shape[0]
    group = 8
    held = coeff_ref[...].reshape(peers * rank, 2 * tile_dev)
    for start in range(0, admissible_ref.shape[1], 512):
        index = admissible_ref[:, start : start + 512]
        low = index & (tile_dev - 1)
        owner = index // tile_dev
        tile = lax.broadcasted_iota(jnp.int32, (2 * tile_dev, 512), 0)
        for c in range(2):
            hot = jnp.where(tile == low + c * tile_dev, 1.0, 0.0).astype(jnp.bfloat16)
            found = jnp.dot(held, hot, preferred_element_type=jnp.float32)
            total = jnp.zeros((rank, 512), jnp.float32)
            for p in range(peers):
                total += jnp.where(owner == p, found[p * rank : (p + 1) * rank], 0.0)
            for j in range(512 // LANES):
                picked_ref[c, start // LANES + j] = total[:, j * LANES : (j + 1) * LANES]
    mixed_ref[...] = jnp.zeros_like(mixed_ref)

    @pl.loop(0, rank)
    def _(r):
        total = [0.0, 0.0]
        for k in range(far_count):
            block = coupling_ref[k, r].astype(jnp.float32)
            total = [total[c] + block * picked_ref[c, k, :, :tile_dev] for c in range(2)]
        for c in range(2):
            mixed_ref[pl.ds(c * rank + r, 1), :tile_dev] = jnp.sum(
                total[c], axis=0, keepdims=True
            )

    @pl.loop(0, tile_dev // group)
    def _(step):
        spread = jnp.where(
            lax.broadcasted_iota(jnp.int32, (2 * LANES, group * LANES), 0) % LANES - step * group
            == lax.broadcasted_iota(jnp.int32, (2 * LANES, group * LANES), 1) // LANES,
            1.0,
            0.0,
        ).astype(jnp.bfloat16)
        far = []
        for c in range(2):
            wide = jnp.dot(
                lookup_operand([mixed_ref[c * rank : (c + 1) * rank, :]]),
                spread,
                preferred_element_type=jnp.float32,
            )
            wide = wide.astype(jnp.bfloat16).astype(jnp.float32)
            far.append(
                jnp.concatenate(
                    [
                        jnp.sum(
                            basis_ref[step * group + j].astype(jnp.float32)
                            * wide[:, j * LANES : (j + 1) * LANES],
                            axis=0,
                            keepdims=True,
                        )
                        for j in range(group)
                    ],
                    axis=0,
                )
            )
        place = pl.ds(pl.multiple_of(step * group, group), group)
        resistance = resistance_ref[place, :]
        reactive = [near_ref[c, place, :] + far[c] for c in range(2)]
        voltage_ref[0, place, :] = resistance * flow_ref[0, place, :] - reactive[1]
        voltage_ref[1, place, :] = resistance * flow_ref[1, place, :] + reactive[0]

    o_ref[...] = jnp.zeros_like(o_ref)

    @pl.loop(0, entry_ref.shape[1] // CHUNK)
    def _(step):
        columns = pl.ds(pl.multiple_of(step * CHUNK, CHUNK), CHUNK)
        tiles = CHUNK // LANES
        voltage = [
            voltage_ref[c, pl.ds(pl.multiple_of(step * tiles, tiles), tiles), :] for c in range(2)
        ]
        voltage = [
            jnp.concatenate([value[j : j + 1] for j in range(tiles)], axis=1) for value in voltage
        ]
        for k in range(entry_ref.shape[0]):
            orient = (2 * sign_ref[k : k + 1, columns] - 1).astype(jnp.float32)
            values = [orient * voltage[c] for c in range(2)]
            o_ref[...] += sums(values, entry_ref[k : k + 1, columns], rows)


def finish_kernel(
    peers, rows, mesh_rows, sums_ref, arrived_ref, asked_ref, answer_ref, port_ref, z_ref, o_ref
):
    asked = row_of(asked_ref, 0, peers)
    arrived = sums([row_of(arrived_ref, c, peers) for c in range(2)], asked, mesh_rows)
    current = answer_ref[0]
    for p in range(1, peers):
        current = current + answer_ref[p]
    products = [
        lax.dot_general(
            current,
            z_ref[part],
            NT,
            precision=lax.Precision.HIGHEST,
            preferred_element_type=jnp.float32,
        )
        for part in range(2)
    ]
    real_part = products[0][2:3] - products[1][3:4]
    imag_part = products[0][3:4] + products[1][2:3]
    ports = sums([real_part, imag_part], port_ref[...], mesh_rows)
    for c in range(2):
        own = slice(c * mesh_rows, (c + 1) * mesh_rows)
        o_ref[c] = sums_ref[c * rows : c * rows + mesh_rows, :] + arrived[own] + ports[own]


def local_call(body, shapes, *arrays, scratch=()):
    return pl.pallas_call(
        body,
        out_shape=shapes,
        scratch_shapes=list(scratch),
        compiler_params=pltpu.CompilerParams(vmem_limit_bytes=VMEM_LIMIT),
    )(*arrays)


def f32(*shape):
    return jax.ShapeDtypeStruct(shape, jnp.float32)


def per_device(
    mesh_current,
    branch_entry,
    branch_sign,
    need_slots,
    resistance,
    near_blocks,
    near_source,
    basis_in,
    coupling,
    basis_out,
    admissible,
    port_mesh,
    port_coupling,
):
    peers = lax.axis_size("clus")
    mesh_dev = mesh_current.shape[1]
    tile_dev, near_count, tile_width = near_blocks.shape[:3]
    rank = basis_in.shape[1]
    ports = port_mesh.shape[0]
    mesh_rows = mesh_dev // LANES
    rows = mesh_rows + peers
    current = mesh_current.reshape(2, mesh_rows, LANES)
    offset = lax.axis_index("clus") * mesh_dev
    port_position = jnp.pad(port_mesh, (0, LANES - ports), constant_values=-1)[None, :] - offset
    impedance = jnp.pad(port_coupling, ((0, 0), (0, LANES - ports), (0, LANES - ports)))

    asked = exchange(jnp.pad(need_slots[:, None, :], ((0, 0), (0, 7), (0, 0))), peers, 0)
    answer = exchange(
        local_call(
            functools.partial(answer_kernel, peers, mesh_rows),
            f32(peers, 8, LANES),
            current,
            asked,
            port_position,
        ),
        peers,
        1,
    )
    flow, coeff = local_call(
        functools.partial(branch_kernel, peers, rows),
        [f32(2, tile_dev, LANES), jax.ShapeDtypeStruct((rank, 2 * tile_dev), jnp.bfloat16)],
        current,
        answer,
        branch_entry,
        branch_sign,
        basis_in.reshape(tile_dev * rank, tile_width),
    )
    all_coeff, near_field = exchange(
        coeff,
        peers,
        2,
        gather=True,
        work=near_work,
        extra=(flow, near_source.reshape(-1, 1), near_blocks),
        made=(f32(2, tile_dev, LANES),),
        scratch=(pltpu.VMEM((2, tile_dev * near_count, LANES), jnp.float32),),
    )
    far_count = admissible.shape[1]
    totals = local_call(
        functools.partial(far_and_collect_kernel, peers, rows),
        f32(2 * rows, LANES),
        all_coeff,
        jnp.pad(admissible.T, ((0, 0), (0, LANES - tile_dev))).reshape(1, -1),
        coupling.transpose(1, 2, 3, 0),
        basis_out,
        near_field,
        flow,
        resistance.reshape(tile_dev, tile_width),
        branch_entry,
        branch_sign,
        scratch=(
            pltpu.VMEM((2, far_count, rank, LANES), jnp.float32),
            pltpu.VMEM((2 * rank, LANES), jnp.float32),
            pltpu.VMEM((2, tile_dev, LANES), jnp.float32),
        ),
    )
    slots = totals.reshape(2, rows, LANES)[:, mesh_rows:].transpose(1, 0, 2)
    arrived = exchange(jnp.pad(slots, ((0, 0), (0, 6), (0, 0))), peers, 3)
    made = local_call(
        functools.partial(finish_kernel, peers, rows, mesh_rows),
        f32(2, mesh_rows, LANES),
        totals,
        arrived,
        asked,
        answer,
        port_position,
        impedance,
    )
    return made.reshape(2, mesh_dev)


def solution(mesh):
    in_specs = (
        P(None, ("groups", "clus")),
        P(None, ("groups", "clus")),
        P(None, ("groups", "clus")),
        P(("groups", "clus"), None),
        P(("groups", "clus")),
        P(("groups", "clus"), None, None, None),
        P(("groups", "clus"), None),
        P(("groups", "clus"), None, None),
        P(("groups", "clus"), None, None, None),
        P(("groups", "clus"), None, None),
        P(("groups", "clus"), None),
        P("groups"),
        P(),
    )
    out_specs = P(None, ("groups", "clus"))
    return jax.shard_map(
        per_device, mesh=mesh, in_specs=in_specs, out_specs=out_specs, check_vma=False
    )
```

```python
import functools

import jax
import jax.numpy as jnp
from jax import lax
from jax.experimental import pallas as pl
from jax.experimental.pallas import tpu as pltpu
from jax.sharding import PartitionSpec as P

LANES = 128
CHUNK = 1024
VMEM_LIMIT = 48 * 1024 * 1024
NT = (((1,), (1,)), ((), ()))


def greet(peers):
    me = lax.axis_index("clus")
    barrier = pltpu.get_barrier_semaphore()

    @pl.loop(1, peers)
    def _(step):
        pl.semaphore_signal(
            barrier,
            inc=1,
            device_id={"clus": lax.rem(me + step, peers)},
            device_id_type=pl.DeviceIdType.MESH,
        )

    pl.semaphore_wait(barrier, peers - 1)


def push(peers, phase, x_ref, o_ref, send_sem, recv_sem, own_sem, gather=False):
    me = lax.axis_index("clus")

    def copy_at(step):
        peer = lax.rem(me + step, peers)
        return pltpu.make_async_remote_copy(
            src_ref=x_ref if gather else x_ref.at[peer],
            dst_ref=o_ref.at[me],
            send_sem=send_sem.at[phase, step],
            recv_sem=recv_sem.at[phase, step],
            device_id={"clus": peer},
            device_id_type=pl.DeviceIdType.MESH,
        )

    @pl.loop(1, peers)
    def _(step):
        copy_at(step).start()

    own = pltpu.make_async_copy(x_ref if gather else x_ref.at[me], o_ref.at[me], own_sem.at[phase])
    own.start()

    def finish():
        own.wait()

        @pl.loop(1, peers)
        def _(step):
            copy_at(step).wait()

    return finish


def near_work(flow_ref, source_ref, blocks_ref, near_ref, picked_ref):
    tile_dev, near_count = blocks_ref.shape[:2]
    count = source_ref.shape[0]
    hot = jnp.where(
        lax.broadcasted_iota(jnp.int32, (count, tile_dev), 1) == source_ref[...], 1.0, 0.0
    ).astype(jnp.bfloat16)
    for c in range(2):
        picked_ref[c] = jnp.dot(
            hot, flow_ref[c].astype(jnp.bfloat16), preferred_element_type=jnp.float32
        )

    @pl.loop(0, tile_dev // 8)
    def _(step):
        rows = []
        for j in range(8):
            tile = step * 8 + j
            total = 0.0
            for k in range(near_count):
                place = pl.ds(tile * near_count + k, 1)
                source = jnp.concatenate([picked_ref[0, place, :], picked_ref[1, place, :]], axis=0)
                total += lax.dot_general(
                    source.astype(jnp.bfloat16),
                    blocks_ref[tile, k],
                    NT,
                    preferred_element_type=jnp.float32,
                )
            rows.append(total)
        for c in range(2):
            near_ref[c, pl.ds(pl.multiple_of(step * 8, 8), 8), :] = jnp.concatenate(
                [row[c : c + 1] for row in rows], axis=0
            )


def split(value):
    high = value.astype(jnp.bfloat16).astype(jnp.float32)
    return high, value - high


def lanes_one_hot(index):
    low = index & (LANES - 1)
    rows = lax.broadcasted_iota(jnp.int32, (LANES, index.shape[1]), 0)
    return jnp.where(rows == low, 1.0, 0.0).astype(jnp.bfloat16)


def rows_mask(index, rows):
    return lax.broadcasted_iota(jnp.int32, (rows, index.shape[1]), 0) == (index >> 7)


def lookup_operand(tables):
    high, low = split(jnp.concatenate(tables, axis=0))
    return jnp.concatenate([high.astype(jnp.bfloat16), low.astype(jnp.bfloat16)], axis=1)


def look_up(operand, index, rows):
    hot = lanes_one_hot(index)
    found = jnp.dot(
        operand, jnp.concatenate([hot, hot], axis=0), preferred_element_type=jnp.float32
    )
    mask = rows_mask(index, rows)
    return [
        jnp.sum(jnp.where(mask, found[c * rows : (c + 1) * rows], 0.0), axis=0, keepdims=True)
        for c in range(2)
    ]


def sums(values, index, rows):
    hot = lanes_one_hot(index)
    mask = rows_mask(index, rows)
    parts = [split(value) for value in values]
    spread = [
        jnp.where(mask, parts[c][part], 0.0).astype(jnp.bfloat16)
        for part in range(2)
        for c in range(2)
    ]
    made = lax.dot_general(
        jnp.concatenate(spread, axis=0), hot, NT, preferred_element_type=jnp.float32
    )
    return made[: 2 * rows] + made[2 * rows :]


def row_of(ref, row, peers):
    return jnp.concatenate([ref[p, row : row + 1, :] for p in range(peers)], axis=1)


def answer_kernel(peers, mesh_rows, current_ref, asked_ref, port_ref, o_ref):
    operand = lookup_operand([current_ref[0], current_ref[1]])
    o_ref[...] = jnp.zeros_like(o_ref)
    asked = look_up(operand, row_of(asked_ref, 0, peers), mesh_rows)
    ports = look_up(operand, port_ref[...], mesh_rows)
    for p in range(peers):
        for c in range(2):
            o_ref[p, c : c + 1, :] = asked[c][:, p * LANES : (p + 1) * LANES]
            o_ref[p, 2 + c : 3 + c, :] = ports[c]


def branch_kernel(
    peers, rows, current_ref, remote_ref, entry_ref, sign_ref, basis_ref, flow_ref, coeff_ref
):
    operand = lookup_operand(
        [
            part
            for c in range(2)
            for part in [current_ref[c]] + [remote_ref[p, c : c + 1, :] for p in range(peers)]
        ]
    )

    @pl.loop(0, entry_ref.shape[1] // CHUNK)
    def _(step):
        columns = pl.ds(pl.multiple_of(step * CHUNK, CHUNK), CHUNK)
        total = [0.0, 0.0]
        for k in range(entry_ref.shape[0]):
            orient = (2 * sign_ref[k : k + 1, columns] - 1).astype(jnp.float32)
            found = look_up(operand, entry_ref[k : k + 1, columns], rows)
            total = [total[c] + orient * found[c] for c in range(2)]
        tiles = CHUNK // LANES
        for c in range(2):
            flow_ref[c, pl.ds(pl.multiple_of(step * tiles, tiles), tiles), :] = jnp.concatenate(
                [total[c][:, j * LANES : (j + 1) * LANES] for j in range(tiles)], axis=0
            )

    tile_dev = flow_ref.shape[1]
    rank = basis_ref.shape[0] // tile_dev
    flows = jnp.concatenate([flow_ref[0], flow_ref[1]], axis=0).astype(jnp.bfloat16)
    part = 8
    total = jnp.zeros((rank, 2 * tile_dev), jnp.float32)
    for start in range(0, tile_dev, part):
        crossed = lax.dot_general(
            basis_ref[start * rank : (start + part) * rank, :],
            flows,
            NT,
            preferred_element_type=jnp.float32,
        )
        lane = lax.broadcasted_iota(jnp.int32, (rank, 2 * tile_dev), 1) & (tile_dev - 1)
        for j in range(part):
            total += jnp.where(lane == start + j, crossed[j * rank : (j + 1) * rank], 0.0)
    coeff_ref[...] = total.astype(jnp.bfloat16)


def far_and_collect_kernel(
    peers,
    rows,
    coeff_ref,
    admissible_ref,
    coupling_ref,
    basis_ref,
    near_ref,
    flow_ref,
    resistance_ref,
    entry_ref,
    sign_ref,
    o_ref,
    picked_ref,
    mixed_ref,
    voltage_ref,
):
    tile_dev, rank = basis_ref.shape[:2]
    far_count = coupling_ref.shape[0]
    group = 8
    held = coeff_ref[...].reshape(peers * rank, 2 * tile_dev)
    for start in range(0, admissible_ref.shape[1], 512):
        index = admissible_ref[:, start : start + 512]
        low = index & (tile_dev - 1)
        owner = index // tile_dev
        tile = lax.broadcasted_iota(jnp.int32, (2 * tile_dev, 512), 0)
        for c in range(2):
            hot = jnp.where(tile == low + c * tile_dev, 1.0, 0.0).astype(jnp.bfloat16)
            found = jnp.dot(held, hot, preferred_element_type=jnp.float32)
            total = jnp.zeros((rank, 512), jnp.float32)
            for p in range(peers):
                total += jnp.where(owner == p, found[p * rank : (p + 1) * rank], 0.0)
            for j in range(512 // LANES):
                picked_ref[c, start // LANES + j] = total[:, j * LANES : (j + 1) * LANES]
    mixed_ref[...] = jnp.zeros_like(mixed_ref)

    @pl.loop(0, rank)
    def _(r):
        total = [0.0, 0.0]
        for k in range(far_count):
            block = coupling_ref[k, r].astype(jnp.float32)
            total = [total[c] + block * picked_ref[c, k, :, :tile_dev] for c in range(2)]
        for c in range(2):
            mixed_ref[pl.ds(c * rank + r, 1), :tile_dev] = jnp.sum(
                total[c], axis=0, keepdims=True
            )

    @pl.loop(0, tile_dev // group)
    def _(step):
        spread = jnp.where(
            lax.broadcasted_iota(jnp.int32, (2 * LANES, group * LANES), 0) % LANES - step * group
            == lax.broadcasted_iota(jnp.int32, (2 * LANES, group * LANES), 1) // LANES,
            1.0,
            0.0,
        ).astype(jnp.bfloat16)
        far = []
        for c in range(2):
            wide = jnp.dot(
                lookup_operand([mixed_ref[c * rank : (c + 1) * rank, :]]),
                spread,
                preferred_element_type=jnp.float32,
            )
            wide = wide.astype(jnp.bfloat16).astype(jnp.float32)
            far.append(
                jnp.concatenate(
                    [
                        jnp.sum(
                            basis_ref[step * group + j].astype(jnp.float32)
                            * wide[:, j * LANES : (j + 1) * LANES],
                            axis=0,
                            keepdims=True,
                        )
                        for j in range(group)
                    ],
                    axis=0,
                )
            )
        place = pl.ds(pl.multiple_of(step * group, group), group)
        resistance = resistance_ref[place, :]
        reactive = [near_ref[c, place, :] + far[c] for c in range(2)]
        voltage_ref[0, place, :] = resistance * flow_ref[0, place, :] - reactive[1]
        voltage_ref[1, place, :] = resistance * flow_ref[1, place, :] + reactive[0]

    o_ref[...] = jnp.zeros_like(o_ref)

    @pl.loop(0, entry_ref.shape[1] // CHUNK)
    def _(step):
        columns = pl.ds(pl.multiple_of(step * CHUNK, CHUNK), CHUNK)
        tiles = CHUNK // LANES
        voltage = [
            voltage_ref[c, pl.ds(pl.multiple_of(step * tiles, tiles), tiles), :] for c in range(2)
        ]
        voltage = [
            jnp.concatenate([value[j : j + 1] for j in range(tiles)], axis=1) for value in voltage
        ]
        for k in range(entry_ref.shape[0]):
            orient = (2 * sign_ref[k : k + 1, columns] - 1).astype(jnp.float32)
            values = [orient * voltage[c] for c in range(2)]
            o_ref[...] += sums(values, entry_ref[k : k + 1, columns], rows)


def finish_kernel(
    peers, rows, mesh_rows, sums_ref, arrived_ref, asked_ref, answer_ref, port_ref, z_ref, o_ref
):
    asked = row_of(asked_ref, 0, peers)
    arrived = sums([row_of(arrived_ref, c, peers) for c in range(2)], asked, mesh_rows)
    current = answer_ref[0]
    for p in range(1, peers):
        current = current + answer_ref[p]
    products = [
        lax.dot_general(
            current,
            z_ref[part],
            NT,
            precision=lax.Precision.HIGHEST,
            preferred_element_type=jnp.float32,
        )
        for part in range(2)
    ]
    real_part = products[0][2:3] - products[1][3:4]
    imag_part = products[0][3:4] + products[1][2:3]
    ports = sums([real_part, imag_part], port_ref[...], mesh_rows)
    for c in range(2):
        own = slice(c * mesh_rows, (c + 1) * mesh_rows)
        o_ref[c] = sums_ref[c * rows : c * rows + mesh_rows, :] + arrived[own] + ports[own]


def whole_kernel(
    peers,
    rows,
    mesh_rows,
    need_ref,
    current_ref,
    port_ref,
    entry_ref,
    sign_ref,
    basis_in_ref,
    source_ref,
    blocks_hbm,
    admissible_ref,
    coupling_hbm,
    basis_out_ref,
    resistance_ref,
    z_ref,
    o_ref,
    asked_ref,
    reply_ref,
    answer_ref,
    flow_ref,
    coeff_ref,
    all_coeff_ref,
    blocks_ref,
    coupling_ref,
    near_ref,
    near_picked_ref,
    picked_ref,
    mixed_ref,
    voltage_ref,
    totals_ref,
    slots_ref,
    arrived_ref,
    send_sem,
    recv_sem,
    own_sem,
    load_sem,
):
    load_blocks = pltpu.make_async_copy(blocks_hbm, blocks_ref, load_sem.at[0])
    load_coupling = pltpu.make_async_copy(coupling_hbm, coupling_ref, load_sem.at[1])
    load_blocks.start()
    load_coupling.start()
    sems = (send_sem, recv_sem, own_sem)
    greet(peers)
    push(peers, 0, need_ref, asked_ref, *sems)()
    answer_kernel(peers, mesh_rows, current_ref, asked_ref, port_ref, reply_ref)
    push(peers, 1, reply_ref, answer_ref, *sems)()
    branch_kernel(
        peers, rows, current_ref, answer_ref, entry_ref, sign_ref, basis_in_ref, flow_ref, coeff_ref
    )
    finish = push(peers, 2, coeff_ref, all_coeff_ref, *sems, gather=True)
    load_blocks.wait()
    near_work(flow_ref, source_ref, blocks_ref, near_ref, near_picked_ref)
    load_coupling.wait()
    finish()
    far_and_collect_kernel(
        peers,
        rows,
        all_coeff_ref,
        admissible_ref,
        coupling_ref,
        basis_out_ref,
        near_ref,
        flow_ref,
        resistance_ref,
        entry_ref,
        sign_ref,
        totals_ref,
        picked_ref,
        mixed_ref,
        voltage_ref,
    )
    slots_ref[...] = jnp.zeros_like(slots_ref)
    for p in range(peers):
        for c in range(2):
            row = c * rows + mesh_rows + p
            slots_ref[p, c : c + 1, :] = totals_ref[row : row + 1, :]
    push(peers, 3, slots_ref, arrived_ref, *sems)()
    finish_kernel(
        peers,
        rows,
        mesh_rows,
        totals_ref,
        arrived_ref,
        asked_ref,
        answer_ref,
        port_ref,
        z_ref,
        o_ref,
    )


def f32(*shape):
    return jax.ShapeDtypeStruct(shape, jnp.float32)


def per_device(
    mesh_current,
    branch_entry,
    branch_sign,
    need_slots,
    resistance,
    near_blocks,
    near_source,
    basis_in,
    coupling,
    basis_out,
    admissible,
    port_mesh,
    port_coupling,
):
    peers = lax.axis_size("clus")
    mesh_dev = mesh_current.shape[1]
    tile_dev, near_count, tile_width = near_blocks.shape[:3]
    rank = basis_in.shape[1]
    ports = port_mesh.shape[0]
    mesh_rows = mesh_dev // LANES
    rows = mesh_rows + peers
    current = mesh_current.reshape(2, mesh_rows, LANES)
    offset = lax.axis_index("clus") * mesh_dev
    port_position = jnp.pad(port_mesh, (0, LANES - ports), constant_values=-1)[None, :] - offset
    impedance = jnp.pad(port_coupling, ((0, 0), (0, LANES - ports), (0, LANES - ports)))

    far_count = admissible.shape[1]
    vmem, hbm = pl.BlockSpec(memory_space=pltpu.VMEM), pl.BlockSpec(memory_space=pl.ANY)
    mixing = coupling.transpose(1, 2, 3, 0)
    message = pltpu.VMEM((peers, 8, LANES), jnp.float32)
    tiles = pltpu.VMEM((2, tile_dev, LANES), jnp.float32)
    made = pl.pallas_call(
        functools.partial(whole_kernel, peers, rows, mesh_rows),
        out_shape=f32(2, mesh_rows, LANES),
        in_specs=[vmem] * 7 + [hbm, vmem, hbm] + [vmem] * 3,
        out_specs=vmem,
        scratch_shapes=[
            pltpu.VMEM((peers, 8, LANES), jnp.int32),
            message,
            message,
            tiles,
            pltpu.VMEM((rank, 2 * tile_dev), jnp.bfloat16),
            pltpu.VMEM((peers, rank, 2 * tile_dev), jnp.bfloat16),
            pltpu.VMEM(near_blocks.shape, near_blocks.dtype),
            pltpu.VMEM(mixing.shape, mixing.dtype),
            tiles,
            pltpu.VMEM((2, tile_dev * near_count, LANES), jnp.float32),
            pltpu.VMEM((2, far_count, rank, LANES), jnp.float32),
            pltpu.VMEM((2 * rank, LANES), jnp.float32),
            tiles,
            pltpu.VMEM((2 * rows, LANES), jnp.float32),
            message,
            message,
            pltpu.SemaphoreType.DMA((4, peers)),
            pltpu.SemaphoreType.DMA((4, peers)),
            pltpu.SemaphoreType.DMA((4,)),
            pltpu.SemaphoreType.DMA((2,)),
        ],
        compiler_params=pltpu.CompilerParams(
            collective_id=0, has_side_effects=True, vmem_limit_bytes=VMEM_LIMIT
        ),
    )(
        jnp.pad(need_slots[:, None, :], ((0, 0), (0, 7), (0, 0))),
        current,
        port_position,
        branch_entry,
        branch_sign,
        basis_in.reshape(tile_dev * rank, tile_width),
        near_source.reshape(-1, 1),
        near_blocks,
        jnp.pad(admissible.T, ((0, 0), (0, LANES - tile_dev))).reshape(1, -1),
        mixing,
        basis_out,
        resistance.reshape(tile_dev, tile_width),
        impedance,
    )
    return made.reshape(2, mesh_dev)


def solution(mesh):
    in_specs = (
        P(None, ("groups", "clus")),
        P(None, ("groups", "clus")),
        P(None, ("groups", "clus")),
        P(("groups", "clus"), None),
        P(("groups", "clus")),
        P(("groups", "clus"), None, None, None),
        P(("groups", "clus"), None),
        P(("groups", "clus"), None, None),
        P(("groups", "clus"), None, None, None),
        P(("groups", "clus"), None, None),
        P(("groups", "clus"), None),
        P("groups"),
        P(),
    )
    out_specs = P(None, ("groups", "clus"))
    return jax.shard_map(
        per_device, mesh=mesh, in_specs=in_specs, out_specs=out_specs, check_vma=False
    )
```

```python
import functools

import jax
import jax.numpy as jnp
from jax import lax
from jax.experimental import pallas as pl
from jax.experimental.pallas import tpu as pltpu
from jax.sharding import PartitionSpec as P

LANES = 128
CHUNK = 1024
VMEM_LIMIT = 48 * 1024 * 1024
NT = (((1,), (1,)), ((), ()))


def greet(peers):
    me = lax.axis_index("clus")
    barrier = pltpu.get_barrier_semaphore()

    @pl.loop(1, peers)
    def _(step):
        pl.semaphore_signal(
            barrier,
            inc=1,
            device_id={"clus": lax.rem(me + step, peers)},
            device_id_type=pl.DeviceIdType.MESH,
        )

    pl.semaphore_wait(barrier, peers - 1)


def push(peers, phase, x_ref, o_ref, send_sem, recv_sem, own_sem, gather=False):
    me = lax.axis_index("clus")

    def copy_at(step):
        peer = lax.rem(me + step, peers)
        return pltpu.make_async_remote_copy(
            src_ref=x_ref if gather else x_ref.at[peer],
            dst_ref=o_ref.at[me],
            send_sem=send_sem.at[phase, step],
            recv_sem=recv_sem.at[phase, step],
            device_id={"clus": peer},
            device_id_type=pl.DeviceIdType.MESH,
        )

    @pl.loop(1, peers)
    def _(step):
        copy_at(step).start()

    own = pltpu.make_async_copy(x_ref if gather else x_ref.at[me], o_ref.at[me], own_sem.at[phase])
    own.start()

    def finish():
        own.wait()

        @pl.loop(1, peers)
        def _(step):
            copy_at(step).wait()

    return finish


def near_work(flow_ref, source_ref, blocks_ref, near_ref, picked_ref):
    tile_dev, near_count = blocks_ref.shape[:2]
    count = source_ref.shape[0]
    hot = jnp.where(
        lax.broadcasted_iota(jnp.int32, (count, tile_dev), 1) == source_ref[...], 1.0, 0.0
    ).astype(jnp.bfloat16)
    for c in range(2):
        picked_ref[c] = jnp.dot(
            hot, flow_ref[c].astype(jnp.bfloat16), preferred_element_type=jnp.float32
        )

    @pl.loop(0, tile_dev // 8)
    def _(step):
        rows = []
        for j in range(8):
            tile = step * 8 + j
            total = 0.0
            for k in range(near_count):
                place = pl.ds(tile * near_count + k, 1)
                source = jnp.concatenate([picked_ref[0, place, :], picked_ref[1, place, :]], axis=0)
                total += lax.dot_general(
                    source.astype(jnp.bfloat16),
                    blocks_ref[tile, k],
                    NT,
                    preferred_element_type=jnp.float32,
                )
            rows.append(total)
        for c in range(2):
            near_ref[c, pl.ds(pl.multiple_of(step * 8, 8), 8), :] = jnp.concatenate(
                [row[c : c + 1] for row in rows], axis=0
            )


def split(value):
    high = value.astype(jnp.bfloat16).astype(jnp.float32)
    return high, value - high


def lanes_one_hot(index):
    low = index & (LANES - 1)
    rows = lax.broadcasted_iota(jnp.int32, (LANES, index.shape[1]), 0)
    return jnp.where(rows == low, 1.0, 0.0).astype(jnp.bfloat16)


def rows_mask(index, rows):
    return lax.broadcasted_iota(jnp.int32, (rows, index.shape[1]), 0) == (index >> 7)


def lookup_operand(tables):
    high, low = split(jnp.concatenate(tables, axis=0))
    return jnp.concatenate([high.astype(jnp.bfloat16), low.astype(jnp.bfloat16)], axis=1)


def look_up(operand, index, rows):
    hot = lanes_one_hot(index)
    found = jnp.dot(
        operand, jnp.concatenate([hot, hot], axis=0), preferred_element_type=jnp.float32
    )
    mask = rows_mask(index, rows)
    return [
        jnp.sum(jnp.where(mask, found[c * rows : (c + 1) * rows], 0.0), axis=0, keepdims=True)
        for c in range(2)
    ]


def sums(values, index, rows):
    hot = lanes_one_hot(index)
    mask = rows_mask(index, rows)
    parts = [split(value) for value in values]
    spread = [
        jnp.where(mask, parts[c][part], 0.0).astype(jnp.bfloat16)
        for part in range(2)
        for c in range(2)
    ]
    made = lax.dot_general(
        jnp.concatenate(spread, axis=0), hot, NT, preferred_element_type=jnp.float32
    )
    return made[: 2 * rows] + made[2 * rows :]


def row_of(ref, row, peers):
    return jnp.concatenate([ref[p, row : row + 1, :] for p in range(peers)], axis=1)


def answer_kernel(peers, mesh_rows, current_ref, asked_ref, port_ref, o_ref):
    operand = lookup_operand([current_ref[0], current_ref[1]])
    o_ref[...] = jnp.zeros_like(o_ref)
    asked = look_up(operand, row_of(asked_ref, 0, peers), mesh_rows)
    ports = look_up(operand, port_ref[...], mesh_rows)
    for p in range(peers):
        for c in range(2):
            o_ref[p, c : c + 1, :] = asked[c][:, p * LANES : (p + 1) * LANES]
            o_ref[p, 2 + c : 3 + c, :] = ports[c]


def branch_kernel(
    peers, rows, current_ref, remote_ref, entry_ref, sign_ref, basis_ref, flow_ref, coeff_ref
):
    operand = lookup_operand(
        [
            part
            for c in range(2)
            for part in [current_ref[c]] + [remote_ref[p, c : c + 1, :] for p in range(peers)]
        ]
    )

    @pl.loop(0, entry_ref.shape[1] // CHUNK)
    def _(step):
        columns = pl.ds(pl.multiple_of(step * CHUNK, CHUNK), CHUNK)
        total = [0.0, 0.0]
        for k in range(entry_ref.shape[0]):
            orient = (2 * sign_ref[k : k + 1, columns] - 1).astype(jnp.float32)
            found = look_up(operand, entry_ref[k : k + 1, columns], rows)
            total = [total[c] + orient * found[c] for c in range(2)]
        tiles = CHUNK // LANES
        for c in range(2):
            flow_ref[c, pl.ds(pl.multiple_of(step * tiles, tiles), tiles), :] = jnp.concatenate(
                [total[c][:, j * LANES : (j + 1) * LANES] for j in range(tiles)], axis=0
            )

    tile_dev = flow_ref.shape[1]
    rank = basis_ref.shape[0] // tile_dev
    flows = jnp.concatenate([flow_ref[0], flow_ref[1]], axis=0).astype(jnp.bfloat16)
    part = 8
    total = jnp.zeros((rank, 2 * tile_dev), jnp.float32)
    for start in range(0, tile_dev, part):
        crossed = lax.dot_general(
            basis_ref[start * rank : (start + part) * rank, :],
            flows,
            NT,
            preferred_element_type=jnp.float32,
        )
        lane = lax.broadcasted_iota(jnp.int32, (rank, 2 * tile_dev), 1) & (tile_dev - 1)
        for j in range(part):
            total += jnp.where(lane == start + j, crossed[j * rank : (j + 1) * rank], 0.0)
    coeff_ref[...] = total.astype(jnp.bfloat16)


def far_and_collect_kernel(
    peers,
    rows,
    coeff_ref,
    admissible_ref,
    coupling_ref,
    basis_ref,
    near_ref,
    flow_ref,
    resistance_ref,
    entry_ref,
    sign_ref,
    o_ref,
    picked_ref,
    mixed_ref,
    voltage_ref,
):
    tile_dev, rank = basis_ref.shape[:2]
    far_count = coupling_ref.shape[0]
    group = 8
    held = coeff_ref[...].reshape(peers * rank, 2 * tile_dev)
    for start in range(0, admissible_ref.shape[1], 512):
        index = admissible_ref[:, start : start + 512]
        low = index & (tile_dev - 1)
        owner = index // tile_dev
        lane = lax.broadcasted_iota(jnp.int32, (1, 512), 1)
        place = low + (lane & tile_dev)
        tile = lax.broadcasted_iota(jnp.int32, (2 * tile_dev, 512), 0)
        hot = jnp.where(tile == place, 1.0, 0.0).astype(jnp.bfloat16)
        found = jnp.dot(held, hot, preferred_element_type=jnp.float32)
        total = jnp.zeros((rank, 512), jnp.float32)
        for p in range(peers):
            total += jnp.where(owner == p, found[p * rank : (p + 1) * rank], 0.0)
        for j in range(512 // LANES):
            for c in range(2):
                half = j * LANES + c * tile_dev
                picked_ref[c, start // LANES + j, :, :tile_dev] = total[:, half : half + tile_dev]
    mixed_ref[...] = jnp.zeros_like(mixed_ref)

    @pl.loop(0, rank)
    def _(r):
        total = [0.0, 0.0]
        for k in range(far_count):
            block = coupling_ref[k, r].astype(jnp.float32)
            total = [total[c] + block * picked_ref[c, k, :, :tile_dev] for c in range(2)]
        for c in range(2):
            mixed_ref[pl.ds(c * rank + r, 1), :tile_dev] = jnp.sum(
                total[c], axis=0, keepdims=True
            )

    @pl.loop(0, tile_dev // group)
    def _(step):
        spread = jnp.where(
            lax.broadcasted_iota(jnp.int32, (2 * LANES, group * LANES), 0) % LANES - step * group
            == lax.broadcasted_iota(jnp.int32, (2 * LANES, group * LANES), 1) // LANES,
            1.0,
            0.0,
        ).astype(jnp.bfloat16)
        far = []
        for c in range(2):
            wide = jnp.dot(
                lookup_operand([mixed_ref[c * rank : (c + 1) * rank, :]]),
                spread,
                preferred_element_type=jnp.float32,
            )
            wide = wide.astype(jnp.bfloat16).astype(jnp.float32)
            far.append(
                jnp.concatenate(
                    [
                        jnp.sum(
                            basis_ref[step * group + j].astype(jnp.float32)
                            * wide[:, j * LANES : (j + 1) * LANES],
                            axis=0,
                            keepdims=True,
                        )
                        for j in range(group)
                    ],
                    axis=0,
                )
            )
        place = pl.ds(pl.multiple_of(step * group, group), group)
        resistance = resistance_ref[place, :]
        reactive = [near_ref[c, place, :] + far[c] for c in range(2)]
        voltage_ref[0, place, :] = resistance * flow_ref[0, place, :] - reactive[1]
        voltage_ref[1, place, :] = resistance * flow_ref[1, place, :] + reactive[0]

    o_ref[...] = jnp.zeros_like(o_ref)

    @pl.loop(0, entry_ref.shape[1] // CHUNK)
    def _(step):
        columns = pl.ds(pl.multiple_of(step * CHUNK, CHUNK), CHUNK)
        tiles = CHUNK // LANES
        voltage = [
            voltage_ref[c, pl.ds(pl.multiple_of(step * tiles, tiles), tiles), :] for c in range(2)
        ]
        voltage = [
            jnp.concatenate([value[j : j + 1] for j in range(tiles)], axis=1) for value in voltage
        ]
        for k in range(entry_ref.shape[0]):
            orient = (2 * sign_ref[k : k + 1, columns] - 1).astype(jnp.float32)
            values = [orient * voltage[c] for c in range(2)]
            o_ref[...] += sums(values, entry_ref[k : k + 1, columns], rows)


def finish_kernel(
    peers, rows, mesh_rows, sums_ref, arrived_ref, asked_ref, answer_ref, port_ref, z_ref, o_ref
):
    asked = row_of(asked_ref, 0, peers)
    arrived = sums([row_of(arrived_ref, c, peers) for c in range(2)], asked, mesh_rows)
    current = answer_ref[0]
    for p in range(1, peers):
        current = current + answer_ref[p]
    products = [
        lax.dot_general(
            current,
            z_ref[part],
            NT,
            precision=lax.Precision.HIGHEST,
            preferred_element_type=jnp.float32,
        )
        for part in range(2)
    ]
    real_part = products[0][2:3] - products[1][3:4]
    imag_part = products[0][3:4] + products[1][2:3]
    ports = sums([real_part, imag_part], port_ref[...], mesh_rows)
    for c in range(2):
        own = slice(c * mesh_rows, (c + 1) * mesh_rows)
        o_ref[c] = sums_ref[c * rows : c * rows + mesh_rows, :] + arrived[own] + ports[own]


def whole_kernel(
    peers,
    rows,
    mesh_rows,
    need_ref,
    current_ref,
    port_ref,
    entry_ref,
    sign_ref,
    basis_in_ref,
    source_ref,
    blocks_hbm,
    admissible_ref,
    coupling_hbm,
    basis_out_ref,
    resistance_ref,
    z_ref,
    o_ref,
    asked_ref,
    reply_ref,
    answer_ref,
    flow_ref,
    coeff_ref,
    all_coeff_ref,
    blocks_ref,
    coupling_ref,
    near_ref,
    near_picked_ref,
    picked_ref,
    mixed_ref,
    voltage_ref,
    totals_ref,
    slots_ref,
    arrived_ref,
    send_sem,
    recv_sem,
    own_sem,
    load_sem,
):
    load_blocks = pltpu.make_async_copy(blocks_hbm, blocks_ref, load_sem.at[0])
    load_coupling = pltpu.make_async_copy(coupling_hbm, coupling_ref, load_sem.at[1])
    load_blocks.start()
    load_coupling.start()
    sems = (send_sem, recv_sem, own_sem)
    greet(peers)
    push(peers, 0, need_ref, asked_ref, *sems)()
    answer_kernel(peers, mesh_rows, current_ref, asked_ref, port_ref, reply_ref)
    push(peers, 1, reply_ref, answer_ref, *sems)()
    branch_kernel(
        peers, rows, current_ref, answer_ref, entry_ref, sign_ref, basis_in_ref, flow_ref, coeff_ref
    )
    finish = push(peers, 2, coeff_ref, all_coeff_ref, *sems, gather=True)
    load_blocks.wait()
    near_work(flow_ref, source_ref, blocks_ref, near_ref, near_picked_ref)
    load_coupling.wait()
    finish()
    far_and_collect_kernel(
        peers,
        rows,
        all_coeff_ref,
        admissible_ref,
        coupling_ref,
        basis_out_ref,
        near_ref,
        flow_ref,
        resistance_ref,
        entry_ref,
        sign_ref,
        totals_ref,
        picked_ref,
        mixed_ref,
        voltage_ref,
    )
    for p in range(peers):
        for c in range(2):
            row = c * rows + mesh_rows + p
            slots_ref[p, c : c + 1, :] = totals_ref[row : row + 1, :]
    push(peers, 3, slots_ref, arrived_ref, *sems)()
    finish_kernel(
        peers,
        rows,
        mesh_rows,
        totals_ref,
        arrived_ref,
        asked_ref,
        answer_ref,
        port_ref,
        z_ref,
        o_ref,
    )


def f32(*shape):
    return jax.ShapeDtypeStruct(shape, jnp.float32)


def per_device(
    mesh_current,
    branch_entry,
    branch_sign,
    need_slots,
    resistance,
    near_blocks,
    near_source,
    basis_in,
    coupling,
    basis_out,
    admissible,
    port_mesh,
    port_coupling,
):
    peers = lax.axis_size("clus")
    mesh_dev = mesh_current.shape[1]
    tile_dev, near_count, tile_width = near_blocks.shape[:3]
    rank = basis_in.shape[1]
    ports = port_mesh.shape[0]
    mesh_rows = mesh_dev // LANES
    rows = mesh_rows + peers
    current = mesh_current.reshape(2, mesh_rows, LANES)
    offset = lax.axis_index("clus") * mesh_dev
    port_position = jnp.pad(port_mesh, (0, LANES - ports), constant_values=-1)[None, :] - offset
    impedance = jnp.pad(port_coupling, ((0, 0), (0, LANES - ports), (0, LANES - ports)))

    far_count = admissible.shape[1]
    vmem, hbm = pl.BlockSpec(memory_space=pltpu.VMEM), pl.BlockSpec(memory_space=pl.ANY)
    mixing = coupling.transpose(1, 2, 3, 0)
    message = pltpu.VMEM((peers, 2, LANES), jnp.float32)
    tiles = pltpu.VMEM((2, tile_dev, LANES), jnp.float32)
    made = pl.pallas_call(
        functools.partial(whole_kernel, peers, rows, mesh_rows),
        out_shape=f32(2, mesh_rows, LANES),
        in_specs=[vmem] * 7 + [hbm, vmem, hbm] + [vmem] * 3,
        out_specs=vmem,
        scratch_shapes=[
            pltpu.VMEM((peers, 1, LANES), jnp.int32),
            pltpu.VMEM((peers, 4, LANES), jnp.float32),
            pltpu.VMEM((peers, 4, LANES), jnp.float32),
            tiles,
            pltpu.VMEM((rank, 2 * tile_dev), jnp.bfloat16),
            pltpu.VMEM((peers, rank, 2 * tile_dev), jnp.bfloat16),
            pltpu.VMEM(near_blocks.shape, near_blocks.dtype),
            pltpu.VMEM(mixing.shape, mixing.dtype),
            tiles,
            pltpu.VMEM((2, tile_dev * near_count, LANES), jnp.float32),
            pltpu.VMEM((2, far_count, rank, LANES), jnp.float32),
            pltpu.VMEM((2 * rank, LANES), jnp.float32),
            tiles,
            pltpu.VMEM((2 * rows, LANES), jnp.float32),
            message,
            message,
            pltpu.SemaphoreType.DMA((4, peers)),
            pltpu.SemaphoreType.DMA((4, peers)),
            pltpu.SemaphoreType.DMA((4,)),
            pltpu.SemaphoreType.DMA((2,)),
        ],
        compiler_params=pltpu.CompilerParams(
            collective_id=0, has_side_effects=True, vmem_limit_bytes=VMEM_LIMIT
        ),
    )(
        need_slots[:, None, :],
        current,
        port_position,
        branch_entry,
        branch_sign,
        basis_in.reshape(tile_dev * rank, tile_width),
        near_source.reshape(-1, 1),
        near_blocks,
        jnp.concatenate([admissible.T, admissible.T], axis=1).reshape(1, -1),
        mixing,
        basis_out,
        resistance.reshape(tile_dev, tile_width),
        impedance,
    )
    return made.reshape(2, mesh_dev)


def solution(mesh):
    in_specs = (
        P(None, ("groups", "clus")),
        P(None, ("groups", "clus")),
        P(None, ("groups", "clus")),
        P(("groups", "clus"), None),
        P(("groups", "clus")),
        P(("groups", "clus"), None, None, None),
        P(("groups", "clus"), None),
        P(("groups", "clus"), None, None),
        P(("groups", "clus"), None, None, None),
        P(("groups", "clus"), None, None),
        P(("groups", "clus"), None),
        P("groups"),
        P(),
    )
    out_specs = P(None, ("groups", "clus"))
    return jax.shard_map(
        per_device, mesh=mesh, in_specs=in_specs, out_specs=out_specs, check_vma=False
    )
```
